256 devices in a mesh: sec: 4 (over y), gz: 4 (over z_lo, core), ta: 16 (over z_hi, x).
Axes of the slice: x: 4, y: 4, z: 8 (z_hi: 4, z_lo: 2; z = z_hi * 2 + z_lo), core: 2. Of those that a mesh axis runs over, the one named last changes fastest.
Arguments:
- source: bfloat16 [16, 8, 6, 8, 32, 128], P('sec', None, None, 'gz', 'ta'), may hold values from -6 to 6
- coarse_links: bfloat16 [8, 6, 8, 32, 9, 64, 128], P('sec', None, 'gz', 'ta'), may hold values from -0.09375 to 0.09375
Outputs:
- correction: float32 [16, 8, 6, 8, 32, 128], P('sec', None, None, 'gz', 'ta')
The draws below stay inside these ranges and needn't reach their ends.
All inputs are finite; a program needn't handle non-finite values.
Results may differ from the reference program's by a relative error of at most 0.0014.
Values may be sent and summed in bfloat16 or wider, within the bound.
No kernel may reach another device: no remote copies, remote signals or barrier semaphores. Data moves between devices by JAX's collectives and lax.ppermute only.
A program may use at most 128 MiB of HBM per device.

```python
import jax
import jax.numpy as jnp
from jax import lax

NV = 64
COLS = 16
NY = 6
SWEEPS = 3
X = 8
Z = 8
T_SIZE = 32


def level_of(own_key, shape, cuts, least, top_value):
    def one(axis_at, blocks):
        steps = jax.random.uniform(jax.random.fold_in(jax.random.fold_in(own_key, 6), axis_at), (blocks,), jnp.float32, least / len(cuts), top_value / len(cuts))
        return jnp.repeat(jnp.exp(steps), shape[axis_at] // blocks).reshape((-1,) + (1,) * (len(shape) - axis_at - 1))

    gain = one(*cuts[0])
    for cut in cuts[1:]:
        gain = gain * one(*cut)
    return gain


def centred(key, shape, width, bound, cuts=(), held_as=jnp.bfloat16):
    result = width * jax.random.normal(key, shape, jnp.float32)
    if cuts:
        result = result * level_of(key, shape, cuts, -0.22, 0.18)
    return jnp.clip(result, -bound, bound).astype(held_as)


def setup_inputs(seed: int = 0) -> dict:
    splits = jax.random.split(jax.random.key(seed), 3)
    return {
        "source": centred(splits[0], (COLS, X, NY, Z, T_SIZE, 2 * NV), 1.0, 6.0, ((0, 4), (3, 4), (4, 16))),
        "coarse_links": centred(splits[1], (X, NY, Z, T_SIZE, 9, NV, 2 * NV), (72 * NV) ** -0.5, 0.09375, ((0, 4), (2, 4), (3, 16))),
    }


def hop_all(vector, coarse_links):
    components = vector.shape[-1] // 2
    width_x = vector.shape[1]

    def one_plane(plane_index):
        def neighbour_plane(offset):
            position = ((plane_index + offset) % width_x).astype(jnp.int32)
            return lax.dynamic_index_in_dim(vector, position, 1, keepdims=False).astype(jnp.float32)

        center = neighbour_plane(0)
        stacked = jnp.stack([center, neighbour_plane(1), neighbour_plane(-1),
                             jnp.roll(center, -1, 1), jnp.roll(center, 1, 1),
                             jnp.roll(center, -1, 2), jnp.roll(center, 1, 2),
                             jnp.roll(center, -1, 3), jnp.roll(center, 1, 3)])
        site_count = center.shape[1] * center.shape[2] * center.shape[3]
        stacked = stacked.reshape(9, center.shape[0], site_count, 2 * components)
        real_part = stacked[..., :components]
        imag_part = stacked[..., components:]
        variants = jnp.stack([jnp.concatenate([real_part, -imag_part], -1),
                              jnp.concatenate([imag_part, real_part], -1)], 1)
        plane_links = lax.dynamic_index_in_dim(coarse_links, plane_index.astype(jnp.int32), 0, keepdims=False)
        plane_links = plane_links.reshape(site_count, 9, components, 2 * components).astype(jnp.float32)
        hopping = jnp.einsum("skin,kvcsn->csvi", plane_links, variants)
        return hopping.reshape(center.shape)

    planes = lax.map(one_plane, jnp.arange(width_x, dtype=jnp.int32))
    return jnp.moveaxis(planes, 0, 1)


def reference(source, coarse_links):
    target = source.astype(jnp.float32)
    iterate = target
    for repeat in range(SWEEPS - 1):
        rounded = lax.optimization_barrier(iterate.astype(jnp.bfloat16))
        iterate = target - hop_all(rounded, coarse_links)
    return iterate
```

```python
import functools

import jax
import jax.numpy as jnp
from jax import lax
from jax.experimental import pallas as pl
from jax.experimental.pallas import tpu as pltpu
from jax.sharding import PartitionSpec as P

BF = jnp.bfloat16
F32 = jnp.float32
VM = pl.BlockSpec(memory_space=pltpu.VMEM)


def permute(array, axis, shift):
    count = lax.axis_size(axis)
    return lax.ppermute(array, axis, [(i, (i + shift) % count) for i in range(count)])


def exchange(faces):
    moved = []
    for number, face in enumerate(faces):
        axis = ("sec", "gz", "ta")[number // 2]
        moved.append(permute(face, axis, -1 if number % 2 == 0 else 1))
    return moved


def site_of(x, y, z, t, ny):
    return ((x * ny + y) * 2 + z) * 2 + t


def store_faces(faces, value, x, y, z, t, ny):
    faces[0 + x][(y * 2 + z) * 2 + t] = value
    faces[2 + z][(x * ny + y) * 2 + t] = value
    faces[4 + t][(x * ny + y) * 2 + z] = value


def pack_kernel(ny, arrived, v_ref, *rest):
    faces, wide = rest[:6], rest[6]
    columns, sites = arrived.shape[0], arrived.shape[1]
    for c in range(columns):
        wide[c * sites:(c + 1) * sites, :] = arrived[c].astype(F32)
    for x in range(2):
        for y in range(ny):
            for z in range(2):
                for t in range(2):
                    site = site_of(x, y, z, t, ny)
                    value = wide[pl.ds(site, columns, stride=sites), :].astype(BF)
                    v_ref[site] = value
                    store_faces(faces, value, x, y, z, t, ny)


def variants(value):
    wide = value.astype(F32)
    half = wide.shape[-1] // 2
    lane = lax.broadcasted_iota(jnp.int32, wide.shape, 1)
    first = jnp.where(lane < half, wide, -wide)
    second = pltpu.roll(wide, half, 1)
    return jnp.concatenate([first, second], 0).astype(BF)


def hop_kernel(ny, last, links, v_ref, *rest):
    near = rest[:6]
    if last:
        source, out, vv = rest[6:]
    else:
        source = v_ref
        v_out, faces, vv = rest[6], rest[7:13], rest[13]
    sites, columns = v_ref.shape[0], v_ref.shape[1]
    half_sites = sites // 2

    def fill(i, carry):
        vv[i] = variants(v_ref[i])
        return carry

    lax.fori_loop(0, sites, fill, 0, unroll=4)
    for number in range(6):
        def fill_near(i, carry, number=number):
            vv[sites + number * half_sites + i] = variants(near[number][i])
            return carry
        lax.fori_loop(0, half_sites, fill_near, 0, unroll=4)

    def row(y, carry):
        up = jnp.where(y == ny - 1, 0, y + 1)
        down = jnp.where(y == 0, ny - 1, y - 1)
        for x in range(2):
            for z in range(2):
                for t in range(2):
                    site = site_of(x, y, z, t, ny)
                    at_x = sites + (y * 2 + z) * 2 + t
                    at_z = sites + 2 * half_sites + (x * ny + y) * 2 + t
                    at_t = sites + 4 * half_sites + (x * ny + y) * 2 + z
                    other_x = site_of(1 - x, y, z, t, ny)
                    other_z = site_of(x, y, 1 - z, t, ny)
                    other_t = site_of(x, y, z, 1 - t, ny)
                    places = [
                        site,
                        other_x if x == 0 else at_x,
                        other_x if x == 1 else at_x + half_sites,
                        site_of(x, up, z, t, ny),
                        site_of(x, down, z, t, ny),
                        other_z if z == 0 else at_z,
                        other_z if z == 1 else at_z + half_sites,
                        other_t if t == 0 else at_t,
                        other_t if t == 1 else at_t + half_sites,
                    ]
                    vectors = jnp.concatenate([vv[p] for p in places], 1)
                    matrix = jnp.concatenate([links[site, k] for k in range(9)], 1)
                    product = lax.dot_general(
                        vectors, matrix, (((1,), (1,)), ((), ())), preferred_element_type=F32
                    )
                    hop = jnp.concatenate([product[:columns], product[columns:]], 1)
                    value = source[site].astype(F32) - hop
                    if last:
                        out[pl.ds(site, columns, stride=sites), :] = value
                    else:
                        value = value.astype(BF)
                        v_out[site] = value
                        store_faces(faces, value, x, y, z, t, ny)
        return carry

    lax.fori_loop(0, ny, row, 0)


def params():
    return pltpu.CompilerParams(vmem_limit_bytes=40 * 1024 * 1024)


def local(ny, source, coarse_links):
    own, planes = source.shape[0], source.shape[1]
    parts = lax.axis_size("sec")
    width = source.shape[-1]
    sites = planes // parts * ny * 4
    columns = own * parts
    links = coarse_links.reshape((sites,) + coarse_links.shape[4:])
    blocks = source.reshape(own, parts, sites, width)
    arrived = lax.all_to_all(blocks, "sec", split_axis=1, concat_axis=0, tiled=True)
    arrived = arrived.reshape(columns, sites, width)
    whole = jax.ShapeDtypeStruct((sites, columns, width), BF)
    face = jax.ShapeDtypeStruct((sites // 2, columns, width), BF)
    v1, *faces = pl.pallas_call(
        functools.partial(pack_kernel, ny),
        out_shape=[whole] + [face] * 6,
        in_specs=[VM],
        out_specs=[VM] * 7,
        scratch_shapes=[pltpu.VMEM((columns * sites, width), F32)],
        compiler_params=params(),
        name="pack",
    )(arrived)
    scratch = [pltpu.VMEM((sites * 4, 2 * columns, width), BF)]
    cost = pl.CostEstimate(
        flops=2 * 9 * sites * 2 * columns * width * width // 2,
        bytes_accessed=links.size * 2,
        transcendentals=0,
    )
    v2, *faces = pl.pallas_call(
        functools.partial(hop_kernel, ny, False),
        out_shape=[whole] + [face] * 6,
        in_specs=[VM] * 8,
        out_specs=[VM] * 7,
        scratch_shapes=scratch,
        compiler_params=params(),
        cost_estimate=cost,
        name="hop_one",
    )(links, v1, *exchange(faces))
    result = pl.pallas_call(
        functools.partial(hop_kernel, ny, True),
        out_shape=jax.ShapeDtypeStruct((columns * sites, width), F32),
        in_specs=[VM] * 9,
        out_specs=VM,
        scratch_shapes=scratch,
        compiler_params=params(),
        cost_estimate=cost,
        name="hop_two",
    )(links, v2, *exchange(faces), v1)
    result = result.reshape(columns, 1, sites, width)
    result = lax.all_to_all(result, "sec", split_axis=0, concat_axis=1, tiled=True)
    return result.reshape(source.shape)


def solution(mesh):
    def whole(source, coarse_links):
        return jax.shard_map(
            functools.partial(local, source.shape[2]),
            mesh=mesh,
            in_specs=(
                P("sec", None, None, "gz", "ta", None),
                P("sec", None, "gz", "ta", None, None, None),
            ),
            out_specs=P("sec", None, None, "gz", "ta", None),
            check_vma=False,
        )(source, coarse_links)

    return whole
```

```python
import functools

import jax
import jax.numpy as jnp
from jax import lax
from jax.experimental import pallas as pl
from jax.experimental.pallas import tpu as pltpu
from jax.sharding import PartitionSpec as P

BF = jnp.bfloat16
F32 = jnp.float32
VM = pl.BlockSpec(memory_space=pltpu.VMEM)
HBM = pl.BlockSpec(memory_space=pl.ANY)
AXES = ("sec", "gz", "ta")


def swap(array, axis, distance):
    count = lax.axis_size(axis)
    return lax.ppermute(array, axis, [(i, i ^ distance) for i in range(count)])


def swap_other(array, axis):
    count = lax.axis_size(axis)
    pairs = [(i, (i + (1 if i % 2 else count - 1)) % count) for i in range(count)]
    return lax.ppermute(array, axis, pairs)


def exchange(faces):
    late = swap_other(faces[5], "ta")
    t_near = swap(faces[4], "ta", 1)
    x_far = swap_other(faces[1], "sec")
    x_near = swap(faces[0], "sec", 1)
    z_far = swap_other(faces[3], "gz")
    z_near = swap(faces[2], "gz", 1)
    return [x_near, x_far, z_near, z_far, t_near], late


def parities():
    return [lax.rem(lax.axis_index(axis), 2) for axis in AXES]


def site_of(x, y, z, t, ny):
    return ((x * ny + y) * 2 + z) * 2 + t


def face_sites(axis, coordinate, i, ny):
    if axis == 0:
        return coordinate * ny * 4 + i
    if axis == 1:
        return (i // 2) * 4 + coordinate * 2 + i % 2
    return i * 2 + coordinate


def write_faces(ny, v_ref, faces):
    odd = parities()
    for axis in range(3):
        for i in range(ny * 4):
            faces[2 * axis][i] = v_ref[face_sites(axis, 1 - odd[axis], i, ny)]
            faces[2 * axis + 1][i] = v_ref[face_sites(axis, odd[axis], i, ny)]


def variants(value):
    wide = value.astype(F32)
    half = wide.shape[-1] // 2
    lane = lax.broadcasted_iota(jnp.int32, wide.shape, 1)
    first = jnp.where(lane < half, wide, -wide)
    second = pltpu.roll(wide, half, 1)
    return jnp.concatenate([first, second], 0).astype(BF)


def fill(target, at, source, count):
    def one(i, carry):
        target[at + i] = variants(source[i])
        return carry

    lax.fori_loop(0, count, one, 0, unroll=8)


def product(vectors, matrices):
    columns = vectors[0].shape[0] // 2
    both = lax.dot_general(
        jnp.concatenate(vectors, 1),
        jnp.concatenate(matrices, 1),
        (((1,), (1,)), ((), ())),
        preferred_element_type=F32,
    )
    return jnp.concatenate([both[:columns], both[columns:]], 1)


def split_kernel(source, *rest):
    outs, sems = rest[:-1], rest[-1]
    me = lax.axis_index("sec")
    copies = []
    for k, out in enumerate(outs):
        copies.append(pltpu.make_async_copy(source.at[:, me ^ k], out, sems.at[k]))
        copies[-1].start()
    for copy in copies:
        copy.wait()


def join_kernel(*refs):
    parts, out, sems = refs[:-2], refs[-2], refs[-1]
    me = lax.axis_index("sec")
    copies = []
    for k, part in enumerate(parts):
        copies.append(pltpu.make_async_copy(part, out.at[:, me ^ k], sems.at[k]))
        copies[-1].start()
    for copy in copies:
        copy.wait()


def pack_kernel(ny, parts, *refs):
    blocks, v_ref, faces, wide = refs[:parts], refs[parts], refs[parts + 1:parts + 7], refs[-1]
    own, sites = blocks[0].shape[0], blocks[0].shape[1]
    me = lax.axis_index("sec")
    for k in range(parts):
        at = (me ^ k) * (own * sites)
        for c in range(own):
            start = pl.multiple_of(at + c * sites, 8)
            wide[pl.ds(start, sites), :] = blocks[k][c].astype(F32)
    for site in range(sites):
        v_ref[site] = wide[pl.ds(site, own * parts, stride=sites), :].astype(BF)
    write_faces(ny, v_ref, faces)


def local_kernel(ny, links, v_ref, source, total, vv):
    sites = v_ref.shape[0]
    fill(vv, 0, v_ref, sites)

    def row(y, carry):
        up = jnp.where(y == ny - 1, 0, y + 1)
        down = jnp.where(y == 0, ny - 1, y - 1)
        for x in range(2):
            for z in range(2):
                for t in range(2):
                    site = site_of(x, y, z, t, ny)
                    terms = [
                        (0, site),
                        (1 + x, site_of(1 - x, y, z, t, ny)),
                        (3, site_of(x, up, z, t, ny)),
                        (4, site_of(x, down, z, t, ny)),
                        (5 + z, site_of(x, y, 1 - z, t, ny)),
                        (7 + t, site_of(x, y, z, 1 - t, ny)),
                    ]
                    hop = product([vv[p] for _, p in terms], [links[site, k] for k, _ in terms])
                    total[site] = source[site].astype(F32) - hop
        return carry

    lax.fori_loop(0, ny, row, 0)


def near_kernel(ny, links, total, *refs):
    near, out, vv = refs[:5], refs[5], refs[6]
    half = near[0].shape[0]
    odd = parities()
    for number in range(5):
        fill(vv, number * half, near[number], half)

    def row(y, carry):
        for side_x in range(2):
            x = 1 - odd[0] if side_x == 0 else odd[0]
            link_x = 1 + (odd[0] if side_x == 0 else 1 - odd[0])
            for side_z in range(2):
                z = 1 - odd[1] if side_z == 0 else odd[1]
                link_z = 5 + (odd[1] if side_z == 0 else 1 - odd[1])
                for side_t in range(2):
                    t = 1 - odd[2] if side_t == 0 else odd[2]
                    site = site_of(x, y, z, t, ny)
                    terms = [
                        (link_x, side_x * half + (y * 2 + z) * 2 + t),
                        (link_z, (2 + side_z) * half + (x * ny + y) * 2 + t),
                    ]
                    if side_t == 0:
                        terms.append((7 + odd[2], 4 * half + (x * ny + y) * 2 + z))
                    hop = product([vv[p] for _, p in terms], [links[site, k] for k, _ in terms])
                    out[site] = total[site] - hop
        return carry

    lax.fori_loop(0, ny, row, 0)


def late_terms(links, late, total, store):
    odd = parities()[2]
    for i in range(late.shape[0]):
        site = i * 2 + odd
        hop = product([variants(late[i])], [links[site, 8 - odd]])
        store(site, total[site] - hop)
        store(i * 2 + 1 - odd, total[i * 2 + 1 - odd])


def late_kernel(ny, links, late, total, v_ref, *faces):
    def store(site, value):
        v_ref[site] = value.astype(BF)

    late_terms(links, late, total, store)
    write_faces(ny, v_ref, faces)


def last_kernel(ny, links, late, total, *refs):
    outs, wide = refs[:-1], refs[-1]
    own, sites = outs[0].shape[0], outs[0].shape[1]
    columns = own * len(outs)

    def store(site, value):
        wide[pl.ds(site, columns, stride=sites), :] = value

    late_terms(links, late, total, store)
    me = lax.axis_index("sec")
    for k, out in enumerate(outs):
        at = (me ^ k) * (own * sites)
        for c in range(own):
            start = pl.multiple_of(at + c * sites, 8)
            out[c] = wide[pl.ds(start, sites), :]


def call(kernel, name, out_shape, inputs, scratch, flops=0, bytes_accessed=0, places=None, out_place=VM):
    several = isinstance(out_shape, list)
    return pl.pallas_call(
        kernel,
        out_shape=out_shape,
        in_specs=places or [VM] * len(inputs),
        out_specs=[out_place] * len(out_shape) if several else out_place,
        scratch_shapes=scratch,
        compiler_params=pltpu.CompilerParams(vmem_limit_bytes=40 * 1024 * 1024),
        cost_estimate=pl.CostEstimate(
            flops=flops, bytes_accessed=bytes_accessed, transcendentals=0
        ),
        name=name,
    )(*inputs)


def local(ny, source, coarse_links):
    own, planes = source.shape[0], source.shape[1]
    parts = lax.axis_size("sec")
    width = source.shape[-1]
    sites = planes // parts * ny * 4
    columns = own * parts
    half = sites // 2
    links = coarse_links.reshape((sites,) + coarse_links.shape[4:])
    shape = jax.ShapeDtypeStruct
    whole = shape((sites, columns, width), BF)
    total_shape = shape((sites, columns, width), F32)
    face = shape((half, columns, width), BF)
    block = shape((own, sites, width), BF)
    wide = pltpu.VMEM((columns * sites, width), F32)
    sems = pltpu.SemaphoreType.DMA((parts,))
    per_term = 2 * sites * 2 * columns * width * width // 2
    link_bytes = links.size * 2 // 9

    blocks = call(
        split_kernel, "split", [block] * parts, [source.reshape(own, parts, sites, width)],
        [sems], bytes_accessed=source.size * 4, places=[HBM],
    )
    blocks = [blocks[0]] + [swap(blocks[k], "sec", k) for k in range(1, parts)]
    v, *faces = call(
        functools.partial(pack_kernel, ny, parts), "pack", [whole] + [face] * 6, blocks,
        [wide], bytes_accessed=source.size * 8,
    )
    first = v
    for sweep in range(2):
        near, late = exchange(faces)
        total = call(
            functools.partial(local_kernel, ny), "local", total_shape, [links, v, first],
            [pltpu.VMEM((sites, 2 * columns, width), BF)],
            flops=6 * per_term, bytes_accessed=6 * link_bytes,
        )
        total = call(
            functools.partial(near_kernel, ny), "near", total_shape, [links, total] + near,
            [pltpu.VMEM((5 * half, 2 * columns, width), BF)],
            flops=5 * per_term // 2, bytes_accessed=5 * link_bytes // 2,
        )
        if sweep == 0:
            v, *faces = call(
                functools.partial(late_kernel, ny), "late", [whole] + [face] * 6,
                [links, late, total], [],
                flops=per_term // 2, bytes_accessed=link_bytes // 2,
            )
        else:
            result = call(
                functools.partial(last_kernel, ny), "last",
                [shape((own, sites, width), F32)] * parts, [links, late, total], [wide],
                flops=per_term // 2, bytes_accessed=link_bytes // 2,
            )
    result = [result[0]] + [swap(result[k], "sec", k) for k in range(1, parts)]
    joined = call(
        join_kernel, "join", shape((own, parts, sites, width), F32), result, [sems],
        bytes_accessed=source.size * 8, out_place=HBM,
    )
    return joined.reshape(source.shape)


def solution(mesh):
    def whole(source, coarse_links):
        return jax.shard_map(
            functools.partial(local, source.shape[2]),
            mesh=mesh,
            in_specs=(
                P("sec", None, None, "gz", "ta", None),
                P("sec", None, "gz", "ta", None, None, None),
            ),
            out_specs=P("sec", None, None, "gz", "ta", None),
            check_vma=False,
        )(source, coarse_links)

    return whole
```

```python
import functools

import jax
import jax.numpy as jnp
from jax import lax
from jax.experimental import pallas as pl
from jax.experimental.pallas import tpu as pltpu
from jax.sharding import PartitionSpec as P

BF = jnp.bfloat16
F32 = jnp.float32
VM = pl.BlockSpec(memory_space=pltpu.VMEM)
ANY = pl.BlockSpec(memory_space=pl.ANY)
HBM = pl.BlockSpec(memory_space=pltpu.HBM)
AXES = ("sec", "gz", "ta")


def swap(array, axis, distance):
    count = lax.axis_size(axis)
    return lax.ppermute(array, axis, [(i, i ^ distance) for i in range(count)])


def swap_other(array, axis):
    count = lax.axis_size(axis)
    pairs = [(i, (i + (1 if i % 2 else count - 1)) % count) for i in range(count)]
    return lax.ppermute(array, axis, pairs)


STARTS = ((3, 1, 2, 0), (2, 5, 3, 1, 0, 4))


def exchange(faces):
    names = AXES[-(len(faces) // 2):]
    order = STARTS[len(faces) == 6]
    moved = []
    for number in order:
        axis, face = names[number // 2], faces[number]
        moved.append(swap_other(face, axis) if number % 2 else swap(face, axis, 1))
    return moved


def parities():
    return [lax.rem(lax.axis_index(axis), 2) for axis in AXES]


def site_of(x, y, z, t, ny):
    return ((x * ny + y) * 2 + z) * 2 + t


def face_sites(axis, coordinate, i, ny):
    if axis == 0:
        return coordinate * ny * 4 + i
    if axis == 1:
        return (i // 2) * 4 + coordinate * 2 + i % 2
    return i * 2 + coordinate


def write_faces(ny, v_ref, faces):
    odd = parities()
    skip = 3 - len(faces) // 2
    for axis in range(skip, 3):
        for i in range(ny * 4):
            near, far = faces[2 * (axis - skip)], faces[2 * (axis - skip) + 1]
            near[i] = v_ref[face_sites(axis, 1 - odd[axis], i, ny)]
            far[i] = v_ref[face_sites(axis, odd[axis], i, ny)]


def variants(value):
    half = value.shape[-1] // 2
    lane = lax.broadcasted_iota(jnp.int32, value.shape, 1)
    wide = value.astype(F32)
    first = jnp.where(lane < half, wide, -wide)
    second = pltpu.roll(wide, half, 1)
    return jnp.concatenate([first, second], 0).astype(BF)


def product(vectors, matrices):
    columns = vectors[0].shape[0] // 2
    both = lax.dot_general(
        jnp.concatenate(vectors, 1),
        jnp.concatenate(matrices, 1),
        (((1,), (1,)), ((), ())),
        preferred_element_type=F32,
    )
    return jnp.concatenate([both[:columns], both[columns:]], 1)


def split_kernel(source, *rest):
    outs, sems = rest[:-1], rest[-1]
    me = lax.axis_index("sec")
    planes = source.shape[1]
    copies = []
    for k, out in enumerate(outs):
        first = 2 * (me ^ k)
        pieces = [
            (lax.rem(first + planes - 1, planes), 1, 0),
            (first, 2, 1),
            (lax.rem(first + 2, planes), 1, 3),
        ]
        for number, (at, count, to) in enumerate(pieces):
            copies.append(
                pltpu.make_async_copy(
                    source.at[:, pl.ds(at, count)], out.at[:, pl.ds(to, count)], sems.at[k, number]
                )
            )
            copies[-1].start()
    for copy in copies:
        copy.wait()


def load_kernel(links, out, sems):
    count = sems.shape[0]
    step = links.shape[0] // count
    copies = []
    for k in range(count):
        part = pl.ds(k * step, step)
        copies.append(pltpu.make_async_copy(links.at[part], out.at[part], sems.at[k]))
        copies[-1].start()
    for copy in copies:
        copy.wait()


def join_kernel(*refs):
    parts, out, sems = refs[:-2], refs[-2], refs[-1]
    me = lax.axis_index("sec")
    copies = []
    for k, part in enumerate(parts):
        copies.append(pltpu.make_async_copy(part, out.at[:, me ^ k], sems.at[k]))
        copies[-1].start()
    for copy in copies:
        copy.wait()


def pack_kernel(ny, parts, *refs):
    blocks, (v_ref, before, after) = refs[:parts], refs[parts + 1:parts + 4]
    faces, wide = refs[parts + 4:-1], refs[-1]
    own, rows = blocks[0].shape[0], blocks[0].shape[1]
    me = lax.axis_index("sec")
    for k in range(parts):
        at = (me ^ k) * (own * rows)
        for c in range(own):
            start = pl.multiple_of(at + c * rows, 8)
            wide[pl.ds(start, rows), :] = blocks[k][c].astype(F32)
    half = rows // 4
    for row in range(rows):
        value = wide[pl.ds(row, own * parts, stride=rows), :].astype(BF)
        if row < half:
            before[row] = value
        elif row < 3 * half:
            v_ref[row - half] = value
        else:
            after[row - 3 * half] = value
    write_faces(ny, v_ref, faces)


def local_kernel(ny, links, v_ref, source, *refs):
    sides, total, vv = refs[:-2], refs[-2], refs[-1]
    sites = v_ref.shape[0]
    for i in range(sites):
        vv[i] = variants(v_ref[i])
    for y in range(ny):
        for x in range(2):
            for z in range(2):
                for t in range(2):
                    site = site_of(x, y, z, t, ny)
                    terms = [
                        (0, site),
                        (1 + x, site_of(1 - x, y, z, t, ny)),
                        (3, site_of(x, (y + 1) % ny, z, t, ny)),
                        (4, site_of(x, (y - 1) % ny, z, t, ny)),
                        (5 + z, site_of(x, y, 1 - z, t, ny)),
                        (7 + t, site_of(x, y, z, 1 - t, ny)),
                    ]
                    vectors = [vv[p] for _, p in terms]
                    matrices = [links[site, k] for k, _ in terms]
                    if sides:
                        vectors.append(variants(sides[x][(y * 2 + z) * 2 + t]))
                        matrices.append(links[site, 2 - x])
                    total[site] = source[site].astype(F32) - product(vectors, matrices)


def near_terms(ny, links, total, moved, store):
    order = STARTS[len(moved) == 6]
    near = [moved[order.index(number)] for number in range(len(order))]
    odd = parities()
    for y in range(ny):
        for side_x in range(2):
            x = 1 - odd[0] if side_x == 0 else odd[0]
            link_x = 1 + (odd[0] if side_x == 0 else 1 - odd[0])
            for side_z in range(2):
                z = 1 - odd[1] if side_z == 0 else odd[1]
                link_z = 5 + (odd[1] if side_z == 0 else 1 - odd[1])
                for side_t in range(2):
                    t = 1 - odd[2] if side_t == 0 else odd[2]
                    link_t = 7 + (odd[2] if side_t == 0 else 1 - odd[2])
                    site = site_of(x, y, z, t, ny)
                    terms = [
                        (link_z, near[-4 + side_z][(x * ny + y) * 2 + t]),
                        (link_t, near[-2 + side_t][(x * ny + y) * 2 + z]),
                    ]
                    if len(near) == 6:
                        terms.append((link_x, near[side_x][(y * 2 + z) * 2 + t]))
                    hop = product([variants(v) for _, v in terms], [links[site, k] for k, _ in terms])
                    store(site, total[site] - hop)


def near_kernel(ny, count, links, total, *refs):
    moved, v_ref, faces = refs[:count], refs[count], refs[count + 1:]

    def store(site, value):
        v_ref[site] = value.astype(BF)

    near_terms(ny, links, total, moved, store)
    write_faces(ny, v_ref, faces)


def last_kernel(ny, count, links, total, *refs):
    moved, outs, wide = refs[:count], refs[count:-1], refs[-1]
    own, sites = outs[0].shape[0], outs[0].shape[1]
    columns = own * len(outs)

    def store(site, value):
        wide[pl.ds(site, columns, stride=sites), :] = value

    near_terms(ny, links, total, moved, store)
    me = lax.axis_index("sec")
    for k, out in enumerate(outs):
        at = (me ^ k) * (own * sites)
        for c in range(own):
            start = pl.multiple_of(at + c * sites, 8)
            out[c] = wide[pl.ds(start, sites), :]


def call(kernel, name, out_shape, inputs, scratch, flops=0, bytes_accessed=0, places=None, out_place=VM):
    several = isinstance(out_shape, list)
    return pl.pallas_call(
        kernel,
        out_shape=out_shape,
        in_specs=places or [VM] * len(inputs),
        out_specs=[out_place] * len(out_shape) if several else out_place,
        scratch_shapes=scratch,
        compiler_params=pltpu.CompilerParams(vmem_limit_bytes=40 * 1024 * 1024),
        cost_estimate=pl.CostEstimate(
            flops=flops, bytes_accessed=bytes_accessed, transcendentals=0
        ),
        name=name,
    )(*inputs)


def local(ny, source, coarse_links):
    own, planes = source.shape[0], source.shape[1]
    parts = lax.axis_size("sec")
    width = source.shape[-1]
    half = ny * 4
    sites = 2 * half
    columns = own * parts
    links = coarse_links.reshape((sites,) + coarse_links.shape[4:])
    shape = jax.ShapeDtypeStruct
    whole = shape((sites, columns, width), BF)
    total_shape = shape((sites, columns, width), F32)
    face = shape((half, columns, width), BF)
    dma = pltpu.SemaphoreType.DMA
    per_term = 2 * sites * 2 * columns * width * width // 2
    link_bytes = links.size * 2 // 9

    blocks = call(
        split_kernel, "split", [shape((own, 4, half, width), BF)] * parts,
        [pltpu.with_memory_space_constraint(source.reshape(own, planes, half, width), pltpu.HBM)],
        [dma((parts, 3))],
        bytes_accessed=source.size * 4, places=[HBM],
    )
    links = call(
        load_kernel, "load", pltpu.VMEM(links.shape, BF),
        [pltpu.with_memory_space_constraint(links, pltpu.HBM)], [dma((8,))],
        bytes_accessed=18 * link_bytes, places=[HBM],
    )
    blocks = [blocks[0]] + [swap(blocks[k], "sec", k) for k in range(1, parts)]
    blocks = [block.reshape(own, 2 * sites, width) for block in blocks]
    v, before, after, *faces = call(
        functools.partial(pack_kernel, ny, parts), "pack", [whole] + [face] * 6, blocks + [links],
        [pltpu.VMEM((columns * 2 * sites, width), F32)], bytes_accessed=source.size * 8,
        places=[VM] * parts + [ANY],
    )
    first, sides = v, [before, after]
    for sweep in range(2):
        moved = exchange(faces)
        total = call(
            functools.partial(local_kernel, ny), "local", total_shape, [links, v, first] + sides,
            [pltpu.VMEM((sites, 2 * columns, width), BF)],
            flops=6 * per_term, bytes_accessed=6 * link_bytes,
        )
        sides = []
        inputs = [links, total] + moved
        cost = dict(flops=3 * per_term, bytes_accessed=3 * link_bytes)
        if sweep == 0:
            v, *faces = call(
                functools.partial(near_kernel, ny, len(moved)), "near", [whole] + [face] * 6,
                inputs, [], **cost,
            )
        else:
            result = call(
                functools.partial(last_kernel, ny, len(moved)), "last",
                [shape((own, sites, width), F32)] * parts, inputs,
                [pltpu.VMEM((columns * sites, width), F32)], **cost,
            )
    result = [result[0]] + [swap(result[k], "sec", k) for k in range(1, parts)]
    joined = call(
        join_kernel, "join", shape((own, parts, sites, width), F32), result, [dma((parts,))],
        bytes_accessed=source.size * 8, out_place=HBM,
    )
    return joined.reshape(source.shape)


def solution(mesh):
    def whole(source, coarse_links):
        return jax.shard_map(
            functools.partial(local, source.shape[2]),
            mesh=mesh,
            in_specs=(
                P("sec", None, None, "gz", "ta", None),
                P("sec", None, "gz", "ta", None, None, None),
            ),
            out_specs=P("sec", None, None, "gz", "ta", None),
            check_vma=False,
        )(source, coarse_links)

    return whole
```

```python
import functools

import jax
import jax.numpy as jnp
from jax import lax
from jax.experimental import pallas as pl
from jax.experimental.pallas import tpu as pltpu
from jax.sharding import PartitionSpec as P

BF = jnp.bfloat16
F32 = jnp.float32
VM = pl.BlockSpec(memory_space=pltpu.VMEM)
ANY = pl.BlockSpec(memory_space=pl.ANY)
HBM = pl.BlockSpec(memory_space=pltpu.HBM)
AXES = ("sec", "gz", "ta")


def swap(array, axis, distance):
    count = lax.axis_size(axis)
    return lax.ppermute(array, axis, [(i, i ^ distance) for i in range(count)])


def swap_other(array, axis):
    count = lax.axis_size(axis)
    pairs = [(i, (i + (1 if i % 2 else count - 1)) % count) for i in range(count)]
    return lax.ppermute(array, axis, pairs)


SWAPS = (0, 2, 1, 3)
STARTS = ((3, 1, 2, 0), (2, 5, 3, 1, 0, 4))


def exchange(faces):
    names = AXES[-(len(faces) // 2):]
    order = STARTS[len(faces) == 6]
    moved = []
    for number in order:
        axis, face = names[number // 2], faces[number]
        moved.append(swap_other(face, axis) if number % 2 else swap(face, axis, 1))
    return moved


def parities():
    return [lax.rem(lax.axis_index(axis), 2) for axis in AXES]


def site_of(x, y, z, t, ny):
    return ((x * ny + y) * 2 + z) * 2 + t


def face_sites(axis, coordinate, i, ny):
    if axis == 0:
        return coordinate * ny * 4 + i
    if axis == 1:
        return (i // 2) * 4 + coordinate * 2 + i % 2
    return i * 2 + coordinate


def write_faces(ny, v_ref, faces):
    odd = parities()
    skip = 3 - len(faces) // 2
    for axis in range(skip, 3):
        for i in range(ny * 4):
            near, far = faces[2 * (axis - skip)], faces[2 * (axis - skip) + 1]
            near[i] = v_ref[face_sites(axis, 1 - odd[axis], i, ny)]
            far[i] = v_ref[face_sites(axis, odd[axis], i, ny)]


def variants(value):
    half = value.shape[-1] // 2
    lane = lax.broadcasted_iota(jnp.int32, value.shape, 1)
    wide = value.astype(F32)
    first = jnp.where(lane < half, wide, -wide)
    second = pltpu.roll(wide, half, 1)
    return jnp.concatenate([first, second], 0).astype(BF)


def product(vectors, matrices):
    columns = vectors[0].shape[0] // 2
    both = lax.dot_general(
        jnp.concatenate(vectors, 1),
        jnp.concatenate(matrices, 1),
        (((1,), (1,)), ((), ())),
        preferred_element_type=F32,
    )
    return jnp.concatenate([both[:columns], both[columns:]], 1)


def split_kernel(source, *rest):
    outs, sems = rest[:-1], rest[-1]
    me = lax.axis_index("sec")
    planes = source.shape[1]
    copies = []
    for number_out, (k, out) in enumerate(zip(SWAPS, outs)):
        first = 2 * (me ^ k)
        pieces = [
            (lax.rem(first + planes - 1, planes), 1, 0),
            (first, 2, 1),
            (lax.rem(first + 2, planes), 1, 3),
        ]
        for number, (at, count, to) in enumerate(pieces):
            copies.append(
                pltpu.make_async_copy(
                    source.at[:, pl.ds(at, count)], out.at[:, pl.ds(to, count)], sems.at[number_out, number]
                )
            )
            copies[-1].start()
    for copy in copies:
        copy.wait()


def load_kernel(links, out, sems):
    count = sems.shape[0]
    step = links.shape[0] // count
    copies = []
    for k in range(count):
        part = pl.ds(k * step, step)
        copies.append(pltpu.make_async_copy(links.at[part], out.at[part], sems.at[k]))
        copies[-1].start()
    for copy in copies:
        copy.wait()


def join_kernel(*refs):
    parts, out, sems = refs[:-2], refs[-2], refs[-1]
    me = lax.axis_index("sec")
    copies = []
    for number, (k, part) in enumerate(zip(SWAPS, parts)):
        copies.append(pltpu.make_async_copy(part, out.at[:, me ^ k], sems.at[number]))
        copies[-1].start()
    for copy in copies:
        copy.wait()


def widen(blocks, wide, pieces):
    own = blocks[0].shape[0]
    count = sum(size for _, size in pieces)
    me = lax.axis_index("sec")
    for k, block in zip(SWAPS, blocks):
        at = (me ^ k) * (own * count)
        for c in range(own):
            to = at + c * count
            for start, size in pieces:
                place = pl.ds(pl.multiple_of(to, 8), size)
                wide[place, :] = block[c, start:start + size].astype(F32)
                to = to + size


def pack_kernel(ny, parts, *refs):
    blocks, v_ref, faces, wide = refs[:parts], refs[parts + 1], refs[parts + 2:-1], refs[-1]
    sites, columns = v_ref.shape[0], v_ref.shape[1]
    widen(blocks, wide, [(sites // 2, sites)])
    for site in range(sites):
        v_ref[site] = wide[pl.ds(site, columns, stride=sites), :].astype(BF)
    write_faces(ny, v_ref, faces)


def local_kernel(ny, links, v_ref, source, *refs):
    sites, columns = v_ref.shape[0], v_ref.shape[1]
    half = sites // 2
    blocks = refs[:-3] if len(refs) > 2 else ()
    total, vv = refs[len(blocks):len(blocks) + 2]
    if blocks:
        wide = refs[-1]
        widen(blocks, wide, [(0, half), (3 * half, half)])
    for i in range(sites):
        vv[i] = variants(v_ref[i])
    for y in range(ny):
        for x in range(2):
            for z in range(2):
                for t in range(2):
                    site = site_of(x, y, z, t, ny)
                    terms = [
                        (0, site),
                        (1 + x, site_of(1 - x, y, z, t, ny)),
                        (3, site_of(x, (y + 1) % ny, z, t, ny)),
                        (4, site_of(x, (y - 1) % ny, z, t, ny)),
                        (5 + z, site_of(x, y, 1 - z, t, ny)),
                        (7 + t, site_of(x, y, z, 1 - t, ny)),
                    ]
                    vectors = [vv[p] for _, p in terms]
                    matrices = [links[site, k] for k, _ in terms]
                    if blocks:
                        row = x * half + (y * 2 + z) * 2 + t
                        vectors.append(variants(wide[pl.ds(row, columns, stride=sites), :]))
                        matrices.append(links[site, 2 - x])
                    total[site] = source[site].astype(F32) - product(vectors, matrices)


def near_terms(ny, links, total, moved, store):
    order = STARTS[len(moved) == 6]
    near = [moved[order.index(number)] for number in range(len(order))]
    odd = parities()
    for y in range(ny):
        for side_x in range(2):
            x = 1 - odd[0] if side_x == 0 else odd[0]
            link_x = 1 + (odd[0] if side_x == 0 else 1 - odd[0])
            for side_z in range(2):
                z = 1 - odd[1] if side_z == 0 else odd[1]
                link_z = 5 + (odd[1] if side_z == 0 else 1 - odd[1])
                for side_t in range(2):
                    t = 1 - odd[2] if side_t == 0 else odd[2]
                    link_t = 7 + (odd[2] if side_t == 0 else 1 - odd[2])
                    site = site_of(x, y, z, t, ny)
                    terms = [
                        (link_z, near[-4 + side_z][(x * ny + y) * 2 + t]),
                        (link_t, near[-2 + side_t][(x * ny + y) * 2 + z]),
                    ]
                    if len(near) == 6:
                        terms.append((link_x, near[side_x][(y * 2 + z) * 2 + t]))
                    hop = product([variants(v) for _, v in terms], [links[site, k] for k, _ in terms])
                    store(site, total[site] - hop)


def near_kernel(ny, count, links, total, *refs):
    moved, v_ref, faces = refs[:count], refs[count], refs[count + 1:]

    def store(site, value):
        v_ref[site] = value.astype(BF)

    near_terms(ny, links, total, moved, store)
    write_faces(ny, v_ref, faces)


def last_kernel(ny, count, links, total, *refs):
    moved, outs, wide = refs[:count], refs[count:-1], refs[-1]
    own, sites = outs[0].shape[0], outs[0].shape[1]
    columns = own * len(outs)

    def store(site, value):
        wide[pl.ds(site, columns, stride=sites), :] = value

    near_terms(ny, links, total, moved, store)
    me = lax.axis_index("sec")
    for k, out in zip(SWAPS, outs):
        at = (me ^ k) * (own * sites)
        for c in range(own):
            start = pl.multiple_of(at + c * sites, 8)
            out[c] = wide[pl.ds(start, sites), :]


def call(kernel, name, out_shape, inputs, scratch, flops=0, bytes_accessed=0, places=None, out_place=VM):
    several = isinstance(out_shape, list)
    return pl.pallas_call(
        kernel,
        out_shape=out_shape,
        in_specs=places or [VM] * len(inputs),
        out_specs=[out_place] * len(out_shape) if several else out_place,
        scratch_shapes=scratch,
        compiler_params=pltpu.CompilerParams(vmem_limit_bytes=40 * 1024 * 1024),
        cost_estimate=pl.CostEstimate(
            flops=flops, bytes_accessed=bytes_accessed, transcendentals=0
        ),
        name=name,
    )(*inputs)


def local(ny, source, coarse_links):
    own, planes = source.shape[0], source.shape[1]
    parts = lax.axis_size("sec")
    width = source.shape[-1]
    half = ny * 4
    sites = 2 * half
    columns = own * parts
    links = coarse_links.reshape((sites,) + coarse_links.shape[4:])
    shape = jax.ShapeDtypeStruct
    whole = shape((sites, columns, width), BF)
    total_shape = shape((sites, columns, width), F32)
    face = shape((half, columns, width), BF)
    dma = pltpu.SemaphoreType.DMA
    per_term = 2 * sites * 2 * columns * width * width // 2
    link_bytes = links.size * 2 // 9

    blocks = call(
        split_kernel, "split", [shape((own, 4, half, width), BF)] * parts,
        [pltpu.with_memory_space_constraint(source.reshape(own, planes, half, width), pltpu.HBM)],
        [dma((parts, 3))],
        bytes_accessed=source.size * 4, places=[HBM],
    )
    links = call(
        load_kernel, "load", pltpu.VMEM(links.shape, BF),
        [pltpu.with_memory_space_constraint(links, pltpu.HBM)], [dma((8,))],
        bytes_accessed=18 * link_bytes, places=[HBM],
    )
    blocks = [blocks[0]] + [swap(block, "sec", k) for k, block in zip(SWAPS[1:], blocks[1:])]
    blocks = [block.reshape(own, 2 * sites, width) for block in blocks]
    wide = pltpu.VMEM((columns * sites, width), F32)
    v, *faces = call(
        functools.partial(pack_kernel, ny, parts), "pack", [whole] + [face] * 4, blocks + [links],
        [wide], bytes_accessed=source.size * 8,
        places=[VM] * parts + [ANY],
    )
    first = v
    for sweep in range(2):
        moved = exchange(faces)
        total = call(
            functools.partial(local_kernel, ny), "local", total_shape, [links, v, first] + blocks,
            [pltpu.VMEM((sites, 2 * columns, width), BF)] + [wide] * (sweep == 0),
            flops=6 * per_term, bytes_accessed=6 * link_bytes,
        )
        blocks = []
        inputs = [links, total] + moved
        cost = dict(flops=3 * per_term, bytes_accessed=3 * link_bytes)
        if sweep == 0:
            v, *faces = call(
                functools.partial(near_kernel, ny, len(moved)), "near", [whole] + [face] * 6,
                inputs, [], **cost,
            )
        else:
            result = call(
                functools.partial(last_kernel, ny, len(moved)), "last",
                [shape((own, sites, width), F32)] * parts, inputs,
                [wide], **cost,
            )
    result = [result[0]] + [swap(part, "sec", k) for k, part in zip(SWAPS[1:], result[1:])]
    joined = call(
        join_kernel, "join", shape((own, parts, sites, width), F32), result, [dma((parts,))],
        bytes_accessed=source.size * 8, out_place=HBM,
    )
    return joined.reshape(source.shape)


def solution(mesh):
    def whole(source, coarse_links):
        return jax.shard_map(
            functools.partial(local, source.shape[2]),
            mesh=mesh,
            in_specs=(
                P("sec", None, None, "gz", "ta", None),
                P("sec", None, "gz", "ta", None, None, None),
            ),
            out_specs=P("sec", None, None, "gz", "ta", None),
            check_vma=False,
        )(source, coarse_links)

    return whole
```

```python
import functools

import jax
import jax.numpy as jnp
from jax import lax
from jax.experimental import pallas as pl
from jax.experimental.pallas import tpu as pltpu
from jax.sharding import PartitionSpec as P

BF = jnp.bfloat16
F32 = jnp.float32
VM = pl.BlockSpec(memory_space=pltpu.VMEM)
ANY = pl.BlockSpec(memory_space=pl.ANY)
HBM = pl.BlockSpec(memory_space=pltpu.HBM)
AXES = ("sec", "gz", "ta")


def swap(array, axis, distance):
    count = lax.axis_size(axis)
    return lax.ppermute(array, axis, [(i, i ^ distance) for i in range(count)])


def swap_other(array, axis):
    count = lax.axis_size(axis)
    pairs = [(i, (i + (1 if i % 2 else count - 1)) % count) for i in range(count)]
    return lax.ppermute(array, axis, pairs)


SWAPS = (0, 2, 1, 3)
FIRST = (5, 3, 4, 2)
EARLY, LATE = (2,), (5, 3, 1, 0, 4)


def exchange(faces, numbers):
    moved = []
    for number in numbers:
        axis, face = AXES[number // 2], faces[number - 6 + len(faces)]
        moved.append(swap_other(face, axis) if number % 2 else swap(face, axis, 1))
    return moved


def parities():
    return [lax.rem(lax.axis_index(axis), 2) for axis in AXES]


def site_of(x, y, z, t, ny):
    return ((x * ny + y) * 2 + z) * 2 + t


def face_sites(axis, coordinate, i, ny):
    if axis == 0:
        return coordinate * ny * 4 + i
    if axis == 1:
        return (i // 2) * 4 + coordinate * 2 + i % 2
    return i * 2 + coordinate


def write_faces(ny, v_ref, faces):
    odd = parities()
    skip = 3 - len(faces) // 2
    for axis in range(skip, 3):
        for i in range(ny * 4):
            near, far = faces[2 * (axis - skip)], faces[2 * (axis - skip) + 1]
            near[i] = v_ref[face_sites(axis, 1 - odd[axis], i, ny)]
            far[i] = v_ref[face_sites(axis, odd[axis], i, ny)]


def variants(value):
    half = value.shape[-1] // 2
    lane = lax.broadcasted_iota(jnp.int32, value.shape, 1)
    wide = value.astype(F32)
    first = jnp.where(lane < half, wide, -wide)
    second = pltpu.roll(wide, half, 1)
    return jnp.concatenate([first, second], 0).astype(BF)


def product(vectors, matrices):
    columns = vectors[0].shape[0] // 2
    both = lax.dot_general(
        jnp.concatenate(vectors, 1),
        jnp.concatenate(matrices, 1),
        (((1,), (1,)), ((), ())),
        preferred_element_type=F32,
    )
    return jnp.concatenate([both[:columns], both[columns:]], 1)


def split_kernel(source, *rest):
    outs, sems = rest[:-1], rest[-1]
    me = lax.axis_index("sec")
    planes = source.shape[1]
    copies = []
    for number_out, (k, out) in enumerate(zip(SWAPS, outs)):
        first = 2 * (me ^ k)
        pieces = [
            (lax.rem(first + planes - 1, planes), 1, 0),
            (first, 2, 1),
            (lax.rem(first + 2, planes), 1, 3),
        ]
        for number, (at, count, to) in enumerate(pieces):
            copies.append(
                pltpu.make_async_copy(
                    source.at[:, pl.ds(at, count)], out.at[:, pl.ds(to, count)], sems.at[number_out, number]
                )
            )
            copies[-1].start()
    for copy in copies:
        copy.wait()


def load_kernel(links, out, sems):
    count = sems.shape[0]
    step = links.shape[0] // count
    copies = []
    for k in range(count):
        part = pl.ds(k * step, step)
        copies.append(pltpu.make_async_copy(links.at[part], out.at[part], sems.at[k]))
        copies[-1].start()
    for copy in copies:
        copy.wait()


def join_kernel(*refs):
    parts, out, sems = refs[:-2], refs[-2], refs[-1]
    me = lax.axis_index("sec")
    copies = []
    for number, (k, part) in enumerate(zip(SWAPS, parts)):
        copies.append(pltpu.make_async_copy(part, out.at[:, me ^ k], sems.at[number]))
        copies[-1].start()
    for copy in copies:
        copy.wait()


def widen(blocks, wide, pieces):
    own = blocks[0].shape[0]
    count = sum(size for _, size in pieces)
    me = lax.axis_index("sec")
    for k, block in zip(SWAPS, blocks):
        at = (me ^ k) * (own * count)
        for c in range(own):
            to = at + c * count
            for start, size in pieces:
                place = pl.ds(pl.multiple_of(to, 8), size)
                wide[place, :] = block[c, start:start + size].astype(F32)
                to = to + size


def pack_kernel(ny, parts, *refs):
    blocks, v_ref, faces, wide = refs[:parts], refs[parts + 1], refs[parts + 2:-1], refs[-1]
    sites, columns = v_ref.shape[0], v_ref.shape[1]
    widen(blocks, wide, [(sites // 2, sites)])
    for site in range(sites):
        v_ref[site] = wide[pl.ds(site, columns, stride=sites), :].astype(BF)
    write_faces(ny, v_ref, faces)


def local_kernel(ny, links, v_ref, source, *refs):
    sites, columns = v_ref.shape[0], v_ref.shape[1]
    half = sites // 2
    blocks = refs[:-3] if len(refs) > 3 else ()
    early = () if blocks else refs[0]
    total, vv = refs[-3:-1] if blocks else refs[-2:]
    odd = parities()[1]
    meets = [odd.astype(F32), (1 - odd).astype(F32)]
    if blocks:
        wide = refs[-1]
        widen(blocks, wide, [(0, half), (3 * half, half)])
    for i in range(sites):
        vv[i] = variants(v_ref[i])
    for y in range(ny):
        for x in range(2):
            for side in range(2):
                z = side
                for t in range(2):
                    site = site_of(x, y, z, t, ny)
                    terms = [
                        (0, site),
                        (1 + x, site_of(1 - x, y, z, t, ny)),
                        (3, site_of(x, (y + 1) % ny, z, t, ny)),
                        (4, site_of(x, (y - 1) % ny, z, t, ny)),
                        (5 + z, site_of(x, y, 1 - z, t, ny)),
                        (7 + t, site_of(x, y, z, 1 - t, ny)),
                    ]
                    vectors = [vv[p] for _, p in terms]
                    matrices = [links[site, k] for k, _ in terms]
                    if blocks:
                        row = x * half + (y * 2 + z) * 2 + t
                        vectors.append(variants(wide[pl.ds(row, columns, stride=sites), :]))
                        matrices.append(links[site, 2 - x])
                    else:
                        vectors.append(variants(early[(x * ny + y) * 2 + t].astype(F32) * meets[z]))
                        matrices.append(links[site, 6 - z])
                    total[site] = source[site].astype(F32) - product(vectors, matrices)


def near_terms(ny, links, total, near, store):
    odd = parities()
    for y in range(ny):
        for side_x in range(2):
            x = 1 - odd[0] if side_x == 0 else odd[0]
            link_x = 1 + (odd[0] if side_x == 0 else 1 - odd[0])
            for side_z in range(2):
                z = 1 - odd[1] if side_z == 0 else odd[1]
                link_z = 5 + (odd[1] if side_z == 0 else 1 - odd[1])
                for side_t in range(2):
                    t = 1 - odd[2] if side_t == 0 else odd[2]
                    link_t = 7 + (odd[2] if side_t == 0 else 1 - odd[2])
                    site = site_of(x, y, z, t, ny)
                    places = [
                        (side_x, link_x, (y * 2 + z) * 2 + t),
                        (2 + side_z, link_z, (x * ny + y) * 2 + t),
                        (4 + side_t, link_t, (x * ny + y) * 2 + z),
                    ]
                    terms = [(k, near[f][i]) for f, k, i in places if f in near]
                    value = total[site]
                    if terms:
                        value = value - product(
                            [variants(v) for _, v in terms], [links[site, k] for k, _ in terms]
                        )
                    store(site, value)


def near_kernel(ny, numbers, links, total, *refs):
    near = dict(zip(numbers, refs))
    v_ref, faces = refs[len(near)], refs[len(near) + 1:]

    def store(site, value):
        v_ref[site] = value.astype(BF)

    near_terms(ny, links, total, near, store)
    write_faces(ny, v_ref, faces)


def last_kernel(ny, numbers, links, total, *refs):
    near = dict(zip(numbers, refs))
    outs, wide = refs[len(near):-1], refs[-1]
    own, sites = outs[0].shape[0], outs[0].shape[1]
    columns = own * len(outs)

    def store(site, value):
        wide[pl.ds(site, columns, stride=sites), :] = value

    near_terms(ny, links, total, near, store)
    me = lax.axis_index("sec")
    for k, out in zip(SWAPS, outs):
        at = (me ^ k) * (own * sites)
        for c in range(own):
            start = pl.multiple_of(at + c * sites, 8)
            out[c] = wide[pl.ds(start, sites), :]


def call(kernel, name, out_shape, inputs, scratch, flops=0, bytes_accessed=0, places=None, out_place=VM):
    several = isinstance(out_shape, list)
    return pl.pallas_call(
        kernel,
        out_shape=out_shape,
        in_specs=places or [VM] * len(inputs),
        out_specs=[out_place] * len(out_shape) if several else out_place,
        scratch_shapes=scratch,
        compiler_params=pltpu.CompilerParams(vmem_limit_bytes=40 * 1024 * 1024),
        cost_estimate=pl.CostEstimate(
            flops=flops, bytes_accessed=bytes_accessed, transcendentals=0
        ),
        name=name,
    )(*inputs)


def local(ny, source, coarse_links):
    own, planes = source.shape[0], source.shape[1]
    parts = lax.axis_size("sec")
    width = source.shape[-1]
    half = ny * 4
    sites = 2 * half
    columns = own * parts
    links = coarse_links.reshape((sites,) + coarse_links.shape[4:])
    shape = jax.ShapeDtypeStruct
    whole = shape((sites, columns, width), BF)
    total_shape = shape((sites, columns, width), F32)
    face = shape((half, columns, width), BF)
    dma = pltpu.SemaphoreType.DMA
    per_term = 2 * sites * 2 * columns * width * width // 2
    link_bytes = links.size * 2 // 9

    blocks = call(
        split_kernel, "split", [shape((own, 4, half, width), BF)] * parts,
        [pltpu.with_memory_space_constraint(source.reshape(own, planes, half, width), pltpu.HBM)],
        [dma((parts, 3))],
        bytes_accessed=source.size * 4, places=[HBM],
    )
    links = call(
        load_kernel, "load", pltpu.VMEM(links.shape, BF),
        [pltpu.with_memory_space_constraint(links, pltpu.HBM)], [dma((8,))],
        bytes_accessed=18 * link_bytes, places=[HBM],
    )
    blocks = [blocks[0]] + [swap(block, "sec", k) for k, block in zip(SWAPS[1:], blocks[1:])]
    blocks = [block.reshape(own, 2 * sites, width) for block in blocks]
    wide = pltpu.VMEM((columns * sites, width), F32)
    v, *faces = call(
        functools.partial(pack_kernel, ny, parts), "pack", [whole] + [face] * 4, blocks + [links],
        [wide], bytes_accessed=source.size * 8,
        places=[VM] * parts + [ANY],
    )
    first = v
    for sweep in range(2):
        moved = exchange(faces, FIRST if sweep == 0 else EARLY)
        late = [] if sweep == 0 else exchange(faces, LATE)
        total = call(
            functools.partial(local_kernel, ny), "local", total_shape, [links, v, first] + (blocks or moved),
            [pltpu.VMEM((sites, 2 * columns, width), BF)] + [wide] * (sweep == 0),
            flops=6 * per_term, bytes_accessed=6 * link_bytes,
        )
        blocks = []
        cost = dict(flops=3 * per_term, bytes_accessed=3 * link_bytes)
        if sweep == 0:
            v, *faces = call(
                functools.partial(near_kernel, ny, FIRST), "near", [whole] + [face] * 6,
                [links, total] + moved, [], **cost,
            )
        else:
            result = call(
                functools.partial(last_kernel, ny, LATE), "last",
                [shape((own, sites, width), F32)] * parts, [links, total] + late, [wide], **cost,
            )
    result = [result[0]] + [swap(part, "sec", k) for k, part in zip(SWAPS[1:], result[1:])]
    joined = call(
        join_kernel, "join", shape((own, parts, sites, width), F32), result, [dma((parts,))],
        bytes_accessed=source.size * 8, out_place=HBM,
    )
    return joined.reshape(source.shape)


def solution(mesh):
    def whole(source, coarse_links):
        return jax.shard_map(
            functools.partial(local, source.shape[2]),
            mesh=mesh,
            in_specs=(
                P("sec", None, None, "gz", "ta", None),
                P("sec", None, "gz", "ta", None, None, None),
            ),
            out_specs=P("sec", None, None, "gz", "ta", None),
            check_vma=False,
        )(source, coarse_links)

    return whole
```

```python
import functools

import jax
import jax.numpy as jnp
from jax import lax
from jax.experimental import pallas as pl
from jax.experimental.pallas import tpu as pltpu
from jax.sharding import PartitionSpec as P

BF = jnp.bfloat16
F32 = jnp.float32
VM = pl.BlockSpec(memory_space=pltpu.VMEM)
ANY = pl.BlockSpec(memory_space=pl.ANY)
HBM = pl.BlockSpec(memory_space=pltpu.HBM)
AXES = ("sec", "gz", "ta")


def swap(array, axis, distance):
    count = lax.axis_size(axis)
    return lax.ppermute(array, axis, [(i, i ^ distance) for i in range(count)])


def swap_other(array, axis):
    count = lax.axis_size(axis)
    pairs = [(i, (i + (1 if i % 2 else count - 1)) % count) for i in range(count)]
    return lax.ppermute(array, axis, pairs)


SWAPS = (0, 2, 1, 3)
FIRST = (5, 3, 4, 2)
EARLY, LATE = (2,), (5, 3, 1, 0, 4)


def exchange(faces, numbers):
    moved = []
    for number in numbers:
        axis, face = AXES[number // 2], faces[number - 6 + len(faces)]
        moved.append(swap_other(face, axis) if number % 2 else swap(face, axis, 1))
    return moved


def parities():
    return [lax.rem(lax.axis_index(axis), 2) for axis in AXES]


def site_of(x, y, z, t, ny):
    return ((x * ny + y) * 2 + z) * 2 + t


def face_sites(axis, coordinate, i, ny):
    if axis == 0:
        return coordinate * ny * 4 + i
    if axis == 1:
        return (i // 2) * 4 + coordinate * 2 + i % 2
    return i * 2 + coordinate


def write_faces(ny, v_ref, faces):
    odd = parities()
    skip = 3 - len(faces) // 2
    for axis in range(skip, 3):
        for i in range(ny * 4):
            near, far = faces[2 * (axis - skip)], faces[2 * (axis - skip) + 1]
            near[i] = v_ref[face_sites(axis, 1 - odd[axis], i, ny)]
            far[i] = v_ref[face_sites(axis, odd[axis], i, ny)]


def variants(value):
    half = value.shape[-1] // 2
    lane = lax.broadcasted_iota(jnp.int32, value.shape, 1)
    wide = value.astype(F32)
    first = jnp.where(lane < half, wide, -wide)
    second = pltpu.roll(wide, half, 1)
    return jnp.concatenate([first, second], 0).astype(BF)


def product(vectors, matrices):
    columns = vectors[0].shape[0] // 2
    both = lax.dot_general(
        jnp.concatenate(vectors, 1),
        jnp.concatenate(matrices, 1),
        (((1,), (1,)), ((), ())),
        preferred_element_type=F32,
    )
    return jnp.concatenate([both[:columns], both[columns:]], 1)


def split_kernel(source, *rest):
    outs, sems = rest[:-1], rest[-1]
    me = lax.axis_index("sec")
    planes = source.shape[1]
    copies = []
    for number_out, (k, out) in enumerate(zip(SWAPS, outs)):
        first = 2 * (me ^ k)
        pieces = [
            (lax.rem(first + planes - 1, planes), 1, 0),
            (first, 2, 1),
            (lax.rem(first + 2, planes), 1, 3),
        ]
        for number, (at, count, to) in enumerate(pieces):
            copies.append(
                pltpu.make_async_copy(
                    source.at[:, pl.ds(at, count)], out.at[:, pl.ds(to, count)], sems.at[number_out, number]
                )
            )
            copies[-1].start()
    for copy in copies:
        copy.wait()


def load_kernel(links, out, sems):
    count = sems.shape[0]
    step = links.shape[0] // count
    copies = []
    for k in range(count):
        part = pl.ds(k * step, step)
        copies.append(pltpu.make_async_copy(links.at[part], out.at[part], sems.at[k]))
        copies[-1].start()
    for copy in copies:
        copy.wait()


def join_kernel(order, *refs):
    parts, out, sems = refs[:len(order)], refs[-2], refs[-1]
    me = lax.axis_index("sec")
    copies = []
    for number, (k, part) in enumerate(zip(order, parts)):
        copies.append(pltpu.make_async_copy(part, out.at[:, me ^ k], sems.at[number]))
        copies[-1].start()
    for copy in copies:
        copy.wait()


def widen(blocks, wide, pieces):
    own = blocks[0].shape[0]
    count = sum(size for _, size in pieces)
    me = lax.axis_index("sec")
    for k, block in zip(SWAPS, blocks):
        at = (me ^ k) * (own * count)
        for c in range(own):
            to = at + c * count
            for start, size in pieces:
                place = pl.ds(pl.multiple_of(to, 8), size)
                wide[place, :] = block[c, start:start + size].astype(F32)
                to = to + size


def pack_kernel(ny, parts, *refs):
    blocks, v_ref, faces, wide = refs[:parts], refs[parts + 1], refs[parts + 2:-1], refs[-1]
    sites, columns = v_ref.shape[0], v_ref.shape[1]
    widen(blocks, wide, [(sites // 2, sites)])
    for site in range(sites):
        v_ref[site] = wide[pl.ds(site, columns, stride=sites), :].astype(BF)
    write_faces(ny, v_ref, faces)


def local_kernel(ny, links, v_ref, source, *refs):
    sites, columns = v_ref.shape[0], v_ref.shape[1]
    half = sites // 2
    blocks = refs[:-3] if len(refs) > 3 else ()
    early = () if blocks else refs[0]
    total, vv = refs[-3:-1] if blocks else refs[-2:]
    odd = parities()[1]
    meets = [odd.astype(F32), (1 - odd).astype(F32)]
    if blocks:
        wide = refs[-1]
        widen(blocks, wide, [(0, half), (3 * half, half)])
    for i in range(sites):
        vv[i] = variants(v_ref[i])
    for y in range(ny):
        for x in range(2):
            for side in range(2):
                z = side
                for t in range(2):
                    site = site_of(x, y, z, t, ny)
                    terms = [
                        (0, site),
                        (1 + x, site_of(1 - x, y, z, t, ny)),
                        (3, site_of(x, (y + 1) % ny, z, t, ny)),
                        (4, site_of(x, (y - 1) % ny, z, t, ny)),
                        (5 + z, site_of(x, y, 1 - z, t, ny)),
                        (7 + t, site_of(x, y, z, 1 - t, ny)),
                    ]
                    vectors = [vv[p] for _, p in terms]
                    matrices = [links[site, k] for k, _ in terms]
                    if blocks:
                        row = x * half + (y * 2 + z) * 2 + t
                        vectors.append(variants(wide[pl.ds(row, columns, stride=sites), :]))
                        matrices.append(links[site, 2 - x])
                    else:
                        vectors.append(variants(early[(x * ny + y) * 2 + t].astype(F32) * meets[z]))
                        matrices.append(links[site, 6 - z])
                    total[site] = source[site].astype(F32) - product(vectors, matrices)


def near_terms(ny, links, total, near, store):
    odd = parities()
    for y in range(ny):
        for side_x in range(2):
            x = 1 - odd[0] if side_x == 0 else odd[0]
            link_x = 1 + (odd[0] if side_x == 0 else 1 - odd[0])
            for side_z in range(2):
                z = 1 - odd[1] if side_z == 0 else odd[1]
                link_z = 5 + (odd[1] if side_z == 0 else 1 - odd[1])
                for side_t in range(2):
                    t = 1 - odd[2] if side_t == 0 else odd[2]
                    link_t = 7 + (odd[2] if side_t == 0 else 1 - odd[2])
                    site = site_of(x, y, z, t, ny)
                    places = [
                        (side_x, link_x, (y * 2 + z) * 2 + t),
                        (2 + side_z, link_z, (x * ny + y) * 2 + t),
                        (4 + side_t, link_t, (x * ny + y) * 2 + z),
                    ]
                    terms = [(k, near[f][i]) for f, k, i in places if f in near]
                    value = total[site]
                    if terms:
                        value = value - product(
                            [variants(v) for _, v in terms], [links[site, k] for k, _ in terms]
                        )
                    store(site, value)


def near_kernel(ny, numbers, links, total, *refs):
    near = dict(zip(numbers, refs))
    v_ref, faces = refs[len(near)], refs[len(near) + 1:]

    def store(site, value):
        v_ref[site] = value.astype(BF)

    near_terms(ny, links, total, near, store)
    write_faces(ny, v_ref, faces)


def last_kernel(ny, numbers, links, total, *refs):
    near = dict(zip(numbers, refs))
    outs, wide = refs[len(near):-1], refs[-1]
    own, sites = outs[0].shape[0], outs[0].shape[1]
    columns = own * len(outs)

    def store(site, value):
        wide[pl.ds(site, columns, stride=sites), :] = value

    near_terms(ny, links, total, near, store)
    me = lax.axis_index("sec")
    for k, out in zip(SWAPS, outs):
        at = (me ^ k) * (own * sites)
        for c in range(own):
            start = pl.multiple_of(at + c * sites, 8)
            out[c] = wide[pl.ds(start, sites), :]


def call(kernel, name, out_shape, inputs, scratch, flops=0, bytes_accessed=0, places=None, out_place=VM, aliases=None):
    several = isinstance(out_shape, list)
    return pl.pallas_call(
        kernel,
        out_shape=out_shape,
        in_specs=places or [VM] * len(inputs),
        out_specs=[out_place] * len(out_shape) if several else out_place,
        scratch_shapes=scratch,
        input_output_aliases=aliases or {},
        compiler_params=pltpu.CompilerParams(vmem_limit_bytes=40 * 1024 * 1024),
        cost_estimate=pl.CostEstimate(
            flops=flops, bytes_accessed=bytes_accessed, transcendentals=0
        ),
        name=name,
    )(*inputs)


def local(ny, source, coarse_links):
    own, planes = source.shape[0], source.shape[1]
    parts = lax.axis_size("sec")
    width = source.shape[-1]
    half = ny * 4
    sites = 2 * half
    columns = own * parts
    links = coarse_links.reshape((sites,) + coarse_links.shape[4:])
    shape = jax.ShapeDtypeStruct
    whole = shape((sites, columns, width), BF)
    total_shape = shape((sites, columns, width), F32)
    face = shape((half, columns, width), BF)
    dma = pltpu.SemaphoreType.DMA
    per_term = 2 * sites * 2 * columns * width * width // 2
    link_bytes = links.size * 2 // 9

    blocks = call(
        split_kernel, "split", [shape((own, 4, half, width), BF)] * parts,
        [pltpu.with_memory_space_constraint(source.reshape(own, planes, half, width), pltpu.HBM)],
        [dma((parts, 3))],
        bytes_accessed=source.size * 4, places=[HBM],
    )
    links = call(
        load_kernel, "load", pltpu.VMEM(links.shape, BF),
        [pltpu.with_memory_space_constraint(links, pltpu.HBM)], [dma((8,))],
        bytes_accessed=18 * link_bytes, places=[HBM],
    )
    blocks = [blocks[0]] + [swap(block, "sec", k) for k, block in zip(SWAPS[1:], blocks[1:])]
    blocks = [block.reshape(own, 2 * sites, width) for block in blocks]
    wide = pltpu.VMEM((columns * sites, width), F32)
    v, *faces = call(
        functools.partial(pack_kernel, ny, parts), "pack", [whole] + [face] * 4, blocks + [links],
        [wide], bytes_accessed=source.size * 8,
        places=[VM] * parts + [ANY],
    )
    first = v
    for sweep in range(2):
        moved = exchange(faces, FIRST if sweep == 0 else EARLY)
        late = [] if sweep == 0 else exchange(faces, LATE)
        total = call(
            functools.partial(local_kernel, ny), "local", total_shape, [links, v, first] + (blocks or moved),
            [pltpu.VMEM((sites, 2 * columns, width), BF)] + [wide] * (sweep == 0),
            flops=6 * per_term, bytes_accessed=6 * link_bytes,
        )
        blocks = []
        cost = dict(flops=3 * per_term, bytes_accessed=3 * link_bytes)
        if sweep == 0:
            v, *faces = call(
                functools.partial(near_kernel, ny, FIRST), "near", [whole] + [face] * 6,
                [links, total] + moved, [], **cost,
            )
        else:
            result = call(
                functools.partial(last_kernel, ny, LATE), "last",
                [shape((own, sites, width), F32)] * parts, [links, total] + late, [wide], **cost,
            )
    result = [result[0]] + [swap(part, "sec", k) for k, part in zip(SWAPS[1:], result[1:])]
    joined = shape((own, parts, sites, width), F32)
    joined = call(
        functools.partial(join_kernel, SWAPS[:2]), "join", joined, result[:2], [dma((2,))],
        bytes_accessed=source.size * 4, out_place=HBM,
    )
    joined = call(
        functools.partial(join_kernel, SWAPS[2:]), "join", shape(joined.shape, F32),
        result[2:] + [joined], [dma((2,))], bytes_accessed=source.size * 4,
        places=[VM] * 2 + [HBM], out_place=HBM, aliases={2: 0},
    )
    return joined.reshape(source.shape)


def solution(mesh):
    def whole(source, coarse_links):
        return jax.shard_map(
            functools.partial(local, source.shape[2]),
            mesh=mesh,
            in_specs=(
                P("sec", None, None, "gz", "ta", None),
                P("sec", None, "gz", "ta", None, None, None),
            ),
            out_specs=P("sec", None, None, "gz", "ta", None),
            check_vma=False,
        )(source, coarse_links)

    return whole
```
